32 devices in a mesh: expert: 8 (over z, y), shard: 4 (over x, core).
Axes of the slice: x: 2, y: 2, z: 4, core: 2. Of those that a mesh axis runs over, the one named last changes fastest.
Arguments:
- tokens: bfloat16 [32768, 768], P(('expert', 'shard')), may hold values from -6 to 6
- expert_route: int32 [32768], P(('expert', 'shard')), may hold values from 0 to 7, as said below
- capacity_slot: int32 [32768], P(('expert', 'shard')), may hold values from 0 to 255, as said below
- buckets: int32 [2047], replicated, may hold values from 0 to 31, as said below
- gain_attn: bfloat16 [768], P('shard'), may hold values from 0.5 to 1.5
- bias_table: bfloat16 [32, 12], P('shard'), may hold values from -4 to 4
- w_query: bfloat16 [768, 768], P('shard'), may hold values from -0.21875 to 0.21875
- w_key: bfloat16 [768, 768], P('shard'), may hold values from -0.21875 to 0.21875
- w_value: bfloat16 [768, 768], P('shard'), may hold values from -0.21875 to 0.21875
- w_output: bfloat16 [768, 768], P('shard'), may hold values from -3.5 to 3.5
- gain_ffn: bfloat16 [768], P('shard'), may hold values from 0.5 to 1.5
- w_router: bfloat16 [768, 8], P('shard'), may hold values from -0.15625 to 0.15625
- w_up: bfloat16 [8, 768, 3072], P('expert', None, 'shard'), may hold values from -0.21875 to 0.21875
- w_down: bfloat16 [8, 3072, 768], P('expert', 'shard'), may hold values from -3 to 3
- cotangent: bfloat16 [32768, 768], P(('expert', 'shard')), may hold values from -6 to 6
Outputs:
- block_out: float32 [32768, 768], P(('expert', 'shard'))
- dtokens: float32 [32768, 768], P(('expert', 'shard'))
- dgain_attn: float32 [768], P('shard')
- dbias_table: float32 [32, 12], P('shard')
- dw_query: float32 [768, 768], P('shard')
- dw_key: float32 [768, 768], P('shard')
- dw_value: float32 [768, 768], P('shard')
- dw_output: float32 [768, 768], P('shard')
- dgain_ffn: float32 [768], P('shard')
- dw_router: float32 [768, 8], P('shard')
- dw_up: float32 [8, 768, 3072], P('expert', None, 'shard')
- dw_down: float32 [8, 3072, 768], P('expert', 'shard')
The draws below stay inside these ranges and needn't reach their ends.
Inputs may be any that keep to these rules, and one draw needn't show every extreme that they name: Within the rows of one device (aligned blocks of 1024 tokens) no two tokens share an expert_route and a capacity_slot; in every block one expert, the same in all blocks, fills all 256 slots, and every expert is named in some block. `capacity_slot`: paired with expert_route as stated there. Entry r + 1023 is the bucket of the offset r = key position minus query position; offsets r <= 0 use the lower half of the buckets, offsets r > 0 the upper half.
All inputs are finite; a program needn't handle non-finite values.
Results may differ from the reference program's by a relative error of at most 0.018.
Values may be sent and summed in bfloat16 or wider, within the bound.
A program may use at most 384 MiB of HBM per device.

```python
import jax
import jax.numpy as jnp
import numpy as np
from jax import lax

D = 768
HEADS = 12
HEAD = 64
F = 3072
BUCKETS = 32
SEQ = 1024
EXPERTS = 8
CAP = 256
TOKENS = 32768


def routing_pair(key):
    blocks = TOKENS // SEQ
    queue_place_count = EXPERTS * CAP
    key_hot, key_level, key_noise, key_order = jax.random.split(key, 4)
    specialist_indicator_matrix = jax.random.randint(key_hot, (), 0, EXPERTS)
    specialist_usage_fraction = jax.random.randint(key_level, (EXPERTS,), 0, 4)
    word_specialist_pick = jnp.arange(queue_place_count, dtype=jnp.int32) // CAP
    gating_jitter_draw = jax.random.randint(key_noise, (blocks, queue_place_count), 0, 8192)
    picked_specialist = jnp.arange(blocks, dtype=jnp.int32)[:, None] % EXPERTS
    offset_attention_addend = specialist_usage_fraction[word_specialist_pick][None, :] * 2048 + jnp.where(word_specialist_pick[None, :] == specialist_indicator_matrix, 65536, 0) + jnp.where(word_specialist_pick[None, :] == picked_specialist, 32768, 0)
    queue_place_rank = (gating_jitter_draw + offset_attention_addend) * queue_place_count + jnp.arange(queue_place_count, dtype=jnp.int32)[None, :]
    chosen = lax_top(queue_place_rank)
    orders = jax.vmap(perm_one)(jax.random.split(key_order, blocks))
    placed = jnp.take_along_axis(chosen, orders, axis=1)
    return ((placed // CAP).reshape(TOKENS).astype(jnp.int32), (placed % CAP).reshape(TOKENS).astype(jnp.int32))


def lax_top(queue_place_rank):
    return jax.lax.top_k(queue_place_rank, SEQ)[1]


def perm_one(key_row):
    return jax.random.permutation(key_row, SEQ)


def draw_expert_route(key, part):
    paired = routing_pair(key)
    return paired[0]


def draw_capacity_slot(key, part):
    paired = routing_pair(key)
    return paired[1]


def draw_buckets(key, part):
    key = jax.random.fold_in(key, 7)
    half_buckets = BUCKETS // 2
    exact_span = half_buckets // 2
    magnitude = np.arange(SEQ)
    scaled_log = np.log(np.maximum(magnitude, 1) / exact_span) / np.log(128 / exact_span) * (half_buckets - exact_span)
    base_table = np.where(magnitude < exact_span, magnitude, np.minimum(exact_span + np.maximum(scaled_log, 0).astype(np.int32), half_buckets - 1)).astype(np.int32)
    offsets = jnp.arange(2 * SEQ - 1, dtype=jnp.int32) - (SEQ - 1)
    bucket_base = jnp.asarray(base_table)[jnp.abs(offsets)]
    jitter = jax.random.randint(key, (2 * SEQ - 1,), 0, 2) * (offsets != 0).astype(jnp.int32)
    return jnp.minimum(bucket_base + jitter, half_buckets - 1) + half_buckets * (offsets > 0).astype(jnp.int32)


def steps_of(rng, shape, shards, smallest, high):
    def one(axis_at, shards_of):
        steps = jax.random.uniform(jax.random.fold_in(jax.random.fold_in(rng, 6), axis_at), (shards_of,), jnp.float32, smallest / len(shards), high / len(shards))
        return jnp.repeat(jnp.exp(steps), shape[axis_at] // shards_of).reshape((-1,) + (1,) * (len(shape) - axis_at - 1))

    gain = one(*shards[0])
    for cut in shards[1:]:
        gain = gain * one(*cut)
    return gain


def normal_values(rng, dims, scale, limit, cuts=(), held_as=jnp.bfloat16):
    drawn = scale * jax.random.normal(rng, dims, jnp.float32)
    if cuts:
        drawn = drawn * steps_of(rng, dims, cuts, -0.22, 0.18)
    return jnp.clip(drawn, -limit, limit).astype(held_as)


def setup_inputs(seed: int = 0) -> dict:
    key_list = jax.random.split(jax.random.key(seed), 16)
    tokens = normal_values(key_list[0], (TOKENS, D), 1.0, 6.0, ((0, 32),))
    expert_route = draw_expert_route(jax.random.fold_in(key_list[15], 71), 0)
    capacity_slot = draw_capacity_slot(jax.random.fold_in(key_list[15], 71), 0)
    buckets = draw_buckets(jax.random.fold_in(key_list[15], 71), 0)
    gain_attn = jnp.clip(1.0 + 0.1 * jax.random.normal(key_list[4], (D,), jnp.float32), 0.5, 1.5).astype(jnp.bfloat16)
    bias_table = normal_values(key_list[5], (BUCKETS, HEADS), 1.0, 4.0, ((0, 4),))
    w_query = normal_values(key_list[6], (D, D), D ** -0.5, 0.21875, ((0, 4),))
    w_key = normal_values(key_list[7], (D, D), D ** -0.5, 0.21875, ((0, 4),))
    w_value = normal_values(key_list[8], (D, D), D ** -0.5, 0.21875, ((0, 4),))
    w_output = normal_values(key_list[9], (D, D), (max(D // 256, 1)) ** -0.5, 3.5, ((0, 4),))
    gain_ffn = jnp.clip(1.0 + 0.1 * jax.random.normal(key_list[10], (D,), jnp.float32), 0.5, 1.5).astype(jnp.bfloat16)
    w_router = normal_values(key_list[11], (D, EXPERTS), (2 * D) ** -0.5, 0.15625, ((0, 4),))
    w_up = normal_values(key_list[12], (EXPERTS, D, F), D ** -0.5, 0.21875, ((0, 8), (2, 4)))
    w_down = normal_values(key_list[13], (EXPERTS, F, D), (1.5 * EXPERTS / F ** 0.5), 3.0, ((0, 8), (1, 4)))
    cotangent = normal_values(key_list[14], (TOKENS, D), 1.0, 6.0, ((0, 32),))
    return {"tokens": tokens, "expert_route": expert_route, "capacity_slot": capacity_slot, "buckets": buckets, "gain_attn": gain_attn, "bias_table": bias_table, "w_query": w_query, "w_key": w_key, "w_value": w_value, "w_output": w_output, "gain_ffn": gain_ffn, "w_router": w_router, "w_up": w_up, "w_down": w_down, "cotangent": cotangent}


@jax.custom_vjp
def low(v):
    return lax.optimization_barrier(v.astype(jnp.bfloat16)).astype(jnp.float32)

@jax.custom_vjp
def low_back(v):
    return v

def low_keep(v):
    return (low(v), None)

def low_pass(kept, grad):
    return (grad,)

def back_keep(v):
    return (v, None)

def back_low(kept, grad):
    return (low(grad),)
low.defvjp(low_keep, low_pass)
low_back.defvjp(back_keep, back_low)
epsilon = 1e-06

def invert(target_row):
    source = jnp.zeros((EXPERTS * CAP,), jnp.int32).at[target_row].set(jnp.arange(SEQ, dtype=jnp.int32))
    filled = jnp.zeros((EXPERTS * CAP,), jnp.bool_).at[target_row].set(True)
    return (source, filled)

def take_rows(table_rows, indices):
    return table_rows[indices]

def reference(tokens, expert_route, capacity_slot, buckets, gain_attn, bias_table, w_query, w_key, w_value, w_output, gain_ffn, w_router, w_up, w_down, cotangent):
    highest = lax.Precision.HIGHEST
    blocks = TOKENS // SEQ
    factor = HEAD ** (-0.5)
    positions = jnp.arange(SEQ, dtype=jnp.int32)
    offsets = positions[None, :] - positions[:, None] + (SEQ - 1)
    bucket_grid = buckets[offsets]
    target = expert_route.reshape(blocks, SEQ) * CAP + capacity_slot.reshape(blocks, SEQ)
    source, filled = jax.vmap(invert)(target)
    picked = (expert_route[:, None] == jnp.arange(EXPERTS, dtype=jnp.int32)[None, :]).astype(jnp.float32)

    def forward(stream, first_gain, bias_weight, wq_full, wk_full, wv_full, wo_full, second_gain, router_w, up_full, down_full):
        first_scale = lax.rsqrt(lax.optimization_barrier(jnp.mean(stream * stream, axis=-1, keepdims=True)) + epsilon)
        normed_one = low(stream * first_scale * first_gain)
        query = low(low_back(jnp.dot(normed_one, wq_full, precision=highest))).reshape(blocks, SEQ, HEADS, HEAD)
        keys = low(low_back(jnp.dot(normed_one, wk_full, precision=highest))).reshape(blocks, SEQ, HEADS, HEAD)
        values = low(low_back(jnp.dot(normed_one, wv_full, precision=highest))).reshape(blocks, SEQ, HEADS, HEAD)
        bias_full = jnp.transpose(bias_weight[bucket_grid], (2, 0, 1))

        def attend(inputs):
            query_seq, key_seq, value_seq = inputs
            raw = low_back(jnp.einsum('qhd,khd->hqk', query_seq, key_seq, precision=highest))
            attn_probs = low(jax.nn.softmax(raw * factor + bias_full, axis=-1))
            return low_back(low(jnp.einsum('hqk,khd->qhd', attn_probs, value_seq, precision=highest)))
        merged = lax.map(jax.checkpoint(attend), (query, keys, values)).reshape(TOKENS, D)
        hidden_one = stream + low_back(jnp.dot(merged, wo_full, precision=highest))
        second_scale = lax.rsqrt(lax.optimization_barrier(jnp.mean(hidden_one * hidden_one, axis=-1, keepdims=True)) + epsilon)
        normed_two = low(hidden_one * second_scale * second_gain)
        logits = low_back(jnp.dot(normed_two, router_w, precision=highest))
        router = jax.nn.softmax(logits, axis=-1)
        gate_prob = lax.optimization_barrier(jnp.sum(router * picked, axis=-1))
        toward = low_back(normed_two).reshape(blocks, SEQ, D)
        buffers = jnp.where(filled[..., None], jax.vmap(take_rows)(toward, source), 0.0)
        grouped = buffers.reshape(blocks, EXPERTS, CAP, D).transpose(1, 0, 2, 3).reshape(EXPERTS, blocks * CAP, D)

        def expert(inputs):
            expert_rows, up_one, down_one = inputs
            pre_act = low_back(jnp.dot(expert_rows, up_one, precision=highest))
            activation = low(jax.nn.gelu(pre_act))
            return low_back(low(jnp.dot(activation, down_one, precision=highest)))
        expert_out = lax.map(jax.checkpoint(expert), (grouped, up_full, down_full))
        back_rows = expert_out.reshape(EXPERTS, blocks, CAP, D).transpose(1, 0, 2, 3).reshape(blocks, EXPERTS * CAP, D)
        chosen = jax.vmap(take_rows)(back_rows, target).reshape(TOKENS, D)
        return hidden_one + gate_prob[:, None] * chosen
    inputs32 = (tokens.astype(jnp.float32), gain_attn.astype(jnp.float32), bias_table.astype(jnp.float32), w_query.astype(jnp.float32), w_key.astype(jnp.float32), w_value.astype(jnp.float32), w_output.astype(jnp.float32), gain_ffn.astype(jnp.float32), w_router.astype(jnp.float32), w_up.astype(jnp.float32), w_down.astype(jnp.float32))
    block_out, pullback = jax.vjp(forward, *inputs32)
    grads = pullback(cotangent.astype(jnp.float32))
    return (block_out, grads[0], grads[1], grads[2], grads[3], grads[4], grads[5], grads[6], grads[7], grads[8], grads[9], grads[10])
```

```python
import functools

import jax
import jax.numpy as jnp
from jax import lax
from jax.experimental import pallas as pl
from jax.experimental.pallas import tpu as pltpu
from jax.sharding import PartitionSpec as P

epsilon = 1e-06
PAIR = 128
SKEW = 128
NT = (((1,), (1,)), ((), ()))
TN = (((0,), (0,)), ((), ()))


def rms_scale(values):
    return lax.rsqrt(jnp.mean(values * values, axis=-1, keepdims=True) + epsilon)


def rms_back(grad_norm, values, factor, gain_vector):
    scaled = grad_norm * gain_vector
    inner_sum = jnp.mean(scaled * values, axis=-1, keepdims=True)
    grad_values = factor * (scaled - values * factor * factor * inner_sum)
    grad_gain = jnp.sum(grad_norm * values * factor, axis=0)
    return (grad_values, grad_gain)


def head_rows(rows, head, head_size, scale):
    lane = lax.broadcasted_iota(jnp.int32, rows.shape, 1)
    mask = jnp.where(lane // head_size == head, scale, 0.0).astype(jnp.float32)
    return (rows.astype(jnp.float32) * mask).astype(jnp.bfloat16)


def forward_kernel(head_size, factor, q_ref, k_ref, v_ref, bias_ref, o_ref, p_ref, skew):
    seq_len = k_ref.shape[0]
    cols = q_ref.shape[0]
    chunk = pl.program_id(1)
    heads = PAIR // head_size

    @pl.when(chunk == 0)
    def _():
        for head in range(heads):
            row = jnp.broadcast_to(bias_ref[head], (SKEW, 2 * seq_len))
            skew[head] = pltpu.roll(row, 0, 1, stride=1, stride_axis=0)

    values_t = v_ref[...].astype(jnp.float32).T.astype(jnp.bfloat16)
    outs = []
    for head in range(heads):
        query = head_rows(q_ref[...], head, head_size, factor)
        raw = lax.dot_general(k_ref[...], query, NT, preferred_element_type=jnp.float32)
        parts = []
        for block in range(seq_len // SKEW):
            start = pl.multiple_of(seq_len - block * SKEW + chunk * cols, SKEW)
            parts.append(
                raw[block * SKEW : (block + 1) * SKEW] + skew[head, :, pl.ds(start, cols)]
            )
        scores = jnp.concatenate(parts, axis=0)
        top = jnp.max(scores, axis=0, keepdims=True)
        exps = jnp.exp(scores - top)
        probs = (exps * (1.0 / jnp.sum(exps, axis=0, keepdims=True))).astype(jnp.bfloat16)
        p_ref[head] = probs
        outs.append(
            jnp.dot(
                values_t[head * head_size : (head + 1) * head_size],
                probs,
                preferred_element_type=jnp.float32,
            )
        )
    o_ref[...] = jnp.concatenate(outs, axis=0).T.astype(jnp.bfloat16)


def backward_kernel(
    head_size,
    factor,
    q_ref,
    k_ref,
    v_ref,
    do_ref,
    p_ref,
    dq_ref,
    dk_ref,
    dv_ref,
    fold_ref,
    dk_sum,
    dv_sum,
    diag,
):
    seq_len = k_ref.shape[0]
    cols = q_ref.shape[0]
    chunk = pl.program_id(1)
    heads = PAIR // head_size

    @pl.when(chunk == 0)
    def _():
        dk_sum[...] = jnp.zeros_like(dk_sum)
        dv_sum[...] = jnp.zeros_like(dv_sum)
        diag[...] = jnp.zeros_like(diag)

    keys_t = (k_ref[...].astype(jnp.float32).T * factor).astype(jnp.bfloat16)
    outs = []
    for head in range(heads):
        grad = head_rows(do_ref[...], head, head_size, 1.0)
        query = head_rows(q_ref[...], head, head_size, factor)
        probs = p_ref[head]
        wide = probs.astype(jnp.float32)
        dprobs = lax.dot_general(v_ref[...], grad, NT, preferred_element_type=jnp.float32)
        terms = wide * dprobs
        dscores = terms - wide * jnp.sum(terms, axis=0, keepdims=True)
        for block in range(seq_len // SKEW):
            start = pl.multiple_of(seq_len - block * SKEW + chunk * cols, SKEW)
            diag[head, :, pl.ds(start, cols)] += dscores[block * SKEW : (block + 1) * SKEW]
        low = dscores.astype(jnp.bfloat16)
        dk_sum[...] += jnp.dot(low, query, preferred_element_type=jnp.float32)
        dv_sum[...] += jnp.dot(probs, grad, preferred_element_type=jnp.float32)
        outs.append(
            jnp.dot(
                keys_t[head * head_size : (head + 1) * head_size],
                low,
                preferred_element_type=jnp.float32,
            )
        )
    dq_ref[...] = jnp.concatenate(outs, axis=0).T.astype(jnp.bfloat16)

    @pl.when(chunk == pl.num_programs(1) - 1)
    def _():
        dk_ref[...] = dk_sum[...].astype(jnp.bfloat16)
        dv_ref[...] = dv_sum[...].astype(jnp.bfloat16)
        for head in range(heads):
            folded = diag[head]
            count = SKEW
            while count > 8:
                count //= 2
                folded = folded[:count] + pltpu.roll(
                    folded[count : 2 * count], 2 * seq_len - count, 1
                )
            fold_ref[head] = folded


def attend_forward(query, keys, values, bias_rows, head_size):
    seq_len, width = query.shape
    heads = PAIR // head_size
    cols = min(256, seq_len)
    part = pl.BlockSpec((cols, PAIR), lambda g, c: (c, g))
    whole = pl.BlockSpec((seq_len, PAIR), lambda g, c: (0, g))
    size = width // head_size * seq_len * seq_len
    return pl.pallas_call(
        functools.partial(forward_kernel, head_size, float(head_size) ** (-0.5)),
        grid=(width // PAIR, seq_len // cols),
        in_specs=[
            part,
            whole,
            whole,
            pl.BlockSpec((heads, 1, 2 * seq_len), lambda g, c: (g, 0, 0)),
        ],
        out_specs=[part, pl.BlockSpec((heads, seq_len, cols), lambda g, c: (g, 0, c))],
        out_shape=[
            jax.ShapeDtypeStruct((seq_len, width), jnp.bfloat16),
            jax.ShapeDtypeStruct((width // head_size, seq_len, seq_len), jnp.bfloat16),
        ],
        scratch_shapes=[pltpu.VMEM((heads, SKEW, 2 * seq_len), jnp.float32)],
        compiler_params=pltpu.CompilerParams(
            dimension_semantics=("arbitrary", "arbitrary"), vmem_limit_bytes=40 * 1024 * 1024
        ),
        cost_estimate=pl.CostEstimate(
            flops=1024 * size, bytes_accessed=2 * size, transcendentals=size
        ),
        name="attend_forward",
    )(query, keys, values, bias_rows)


def attend_backward(query, keys, values, grad, probs, head_size, base, width):
    seq_len = query.shape[0]
    heads = PAIR // head_size
    cols = min(256, seq_len)
    skip = base // PAIR
    part = pl.BlockSpec((cols, PAIR), lambda g, c: (c, g + skip))
    whole = pl.BlockSpec((seq_len, PAIR), lambda g, c: (0, g + skip))
    part_out = pl.BlockSpec((cols, PAIR), lambda g, c: (c, g))
    whole_out = pl.BlockSpec((seq_len, PAIR), lambda g, c: (0, g))
    size = width // head_size * seq_len * seq_len
    narrow = jax.ShapeDtypeStruct((seq_len, width), jnp.bfloat16)
    return pl.pallas_call(
        functools.partial(backward_kernel, head_size, float(head_size) ** (-0.5)),
        grid=(width // PAIR, seq_len // cols),
        in_specs=[
            part,
            whole,
            whole,
            part,
            pl.BlockSpec((heads, seq_len, cols), lambda g, c: (g + skip, 0, c)),
        ],
        out_specs=[
            part_out,
            whole_out,
            whole_out,
            pl.BlockSpec((heads, 8, 2 * seq_len), lambda g, c: (g, 0, 0)),
        ],
        out_shape=[
            narrow,
            narrow,
            narrow,
            jax.ShapeDtypeStruct((width // head_size, 8, 2 * seq_len), jnp.float32),
        ],
        scratch_shapes=[
            pltpu.VMEM((seq_len, PAIR), jnp.float32),
            pltpu.VMEM((seq_len, PAIR), jnp.float32),
            pltpu.VMEM((heads, SKEW, 2 * seq_len), jnp.float32),
        ],
        compiler_params=pltpu.CompilerParams(
            dimension_semantics=("arbitrary", "arbitrary"), vmem_limit_bytes=40 * 1024 * 1024
        ),
        cost_estimate=pl.CostEstimate(
            flops=2048 * size, bytes_accessed=2 * size, transcendentals=0
        ),
        name="attend_backward",
    )(query, keys, values, grad, probs)


def expert_forward(expert_rows, up_weights, down_weights):
    pre_act = jnp.einsum(
        "erd,edf->erf", expert_rows, up_weights, preferred_element_type=jnp.float32
    )
    activation = jax.nn.gelu(pre_act).astype(jnp.bfloat16)
    expert_out = jnp.einsum(
        "erf,efd->erd", activation, down_weights, preferred_element_type=jnp.float32
    )
    return (pre_act.astype(jnp.bfloat16), activation, expert_out)


def to_experts(rows, n_expert, local_experts, capacity):
    width = rows.shape[-1]
    sent = rows.reshape(n_expert, local_experts * capacity, width)
    got = lax.all_to_all(sent, "expert", split_axis=0, concat_axis=0, tiled=True)
    got = got.reshape(n_expert, local_experts, capacity, width)
    return got.transpose(1, 0, 2, 3).reshape(local_experts, n_expert * capacity, width)


def from_experts(rows, n_expert, local_experts, capacity):
    width = rows.shape[-1]
    sent = rows.reshape(local_experts, n_expert, capacity, width).transpose(1, 0, 2, 3)
    sent = sent.reshape(n_expert, local_experts * capacity, width)
    got = lax.all_to_all(sent, "expert", split_axis=0, concat_axis=0, tiled=True)
    return got.reshape(n_expert * local_experts * capacity, width)


def packed(columns, rows):
    widths = [column.shape[1] for column in columns]
    spare = -sum(widths) % 128
    parts = [column.astype(jnp.bfloat16) for column in columns]
    if spare:
        parts.append(jnp.zeros((rows, spare), jnp.bfloat16))
    return jnp.concatenate(parts, axis=1)


def as_column(values, rows, groups):
    values = values.reshape(groups, -1)
    spare = rows // groups - values.shape[1]
    return jnp.pad(values, ((0, 0), (0, spare))).reshape(rows, 1)


def summed_blocks(blocks, axis):
    got = lax.all_to_all(blocks, axis, split_axis=0, concat_axis=0, tiled=True)
    return jnp.sum(got.astype(jnp.float32), axis=0).astype(jnp.bfloat16)


def total_over_experts(rows, n_expert):
    count, width = rows.shape
    mine = summed_blocks(rows.reshape(n_expert, count // n_expert, width), "expert")
    return lax.all_gather(mine, "expert", axis=0, tiled=True).astype(jnp.float32)


def shards(
    tokens,
    expert_route,
    capacity_slot,
    buckets,
    gain_attn,
    bias_table,
    w_query,
    w_key,
    w_value,
    w_output,
    gain_ffn,
    w_router,
    w_up,
    w_down,
    cotangent,
):
    seq_len, model_width = tokens.shape
    n_expert = lax.axis_size("expert")
    n_shard = lax.axis_size("shard")
    held = w_query.shape[0]
    head_count = bias_table.shape[1]
    head_size = model_width // head_count
    bucket_count = bias_table.shape[0] * n_shard
    experts = w_router.shape[1]
    local_experts = w_up.shape[0]
    capacity = 2 * seq_len // experts
    first = packed(
        [w_query, w_key, w_value, gain_attn[:, None], as_column(bias_table, held, 1)], held
    )
    first = lax.all_gather(first, "shard", axis=0, tiled=True)
    first, w_output = lax.optimization_barrier((first, w_output))
    second = packed([w_output, w_router, gain_ffn[:, None]], held)
    second = lax.all_gather(second, "shard", axis=0, tiled=True)
    full_up = lax.all_gather(w_up, "shard", axis=2, tiled=True)
    full_down = lax.all_gather(w_down, "shard", axis=1, tiled=True)
    query_w = first[:, :model_width]
    key_w = first[:, model_width : 2 * model_width]
    value_w = first[:, 2 * model_width : 3 * model_width]
    gain_one = first[:, 3 * model_width].astype(jnp.float32)
    table_full = first[:, 3 * model_width + 1].reshape(n_shard, held)[:, : bias_table.size]
    table_full = table_full.reshape(bucket_count, head_count)
    output_w = second[:, :model_width]
    router_w = second[:, model_width : model_width + experts]
    gain_two = second[:, model_width + experts].astype(jnp.float32)

    ordered = jnp.concatenate([buckets[:1], buckets[::-1]])
    bucket_onehot = (
        ordered[:, None] == jnp.arange(bucket_count, dtype=jnp.int32)[None, :]
    ).astype(jnp.bfloat16)
    bias_rows = jnp.einsum(
        "rb,bh->hr", bucket_onehot, table_full, preferred_element_type=jnp.float32
    )[:, None, :]
    target = expert_route * capacity + capacity_slot
    placing = (
        jnp.arange(experts * capacity, dtype=jnp.int32)[:, None] == target[None, :]
    ).astype(jnp.bfloat16)

    stream = tokens.astype(jnp.float32)
    first_scale = rms_scale(stream)
    normed_one = (stream * first_scale * gain_one).astype(jnp.bfloat16)
    query = jnp.dot(normed_one, query_w, preferred_element_type=jnp.float32).astype(jnp.bfloat16)
    keys = jnp.dot(normed_one, key_w, preferred_element_type=jnp.float32).astype(jnp.bfloat16)
    values = jnp.dot(normed_one, value_w, preferred_element_type=jnp.float32).astype(jnp.bfloat16)
    merged, probs = attend_forward(query, keys, values, bias_rows, head_size)
    hidden_one = stream + jnp.dot(merged, output_w, preferred_element_type=jnp.float32)
    second_scale = rms_scale(hidden_one)
    normed_two = (hidden_one * second_scale * gain_two).astype(jnp.bfloat16)

    outgoing = jnp.dot(placing, normed_two, preferred_element_type=jnp.float32)
    arrived = to_experts(outgoing.astype(jnp.bfloat16), n_expert, local_experts, capacity)

    logits = jnp.dot(normed_two, router_w, preferred_element_type=jnp.float32)
    router = jax.nn.softmax(logits, axis=-1)
    picked = (expert_route[:, None] == jnp.arange(experts, dtype=jnp.int32)[None, :]).astype(
        jnp.float32
    )
    gate_prob = jnp.sum(router * picked, axis=-1)
    grad_mixed = cotangent.astype(jnp.float32)
    grad_chosen = (gate_prob[:, None] * grad_mixed).astype(jnp.bfloat16)
    outgoing_grad = jnp.dot(placing, grad_chosen, preferred_element_type=jnp.float32)
    arrived_grad = to_experts(
        outgoing_grad.astype(jnp.bfloat16), n_expert, local_experts, capacity
    )

    pre_act, activation, whole_out = expert_forward(arrived, full_up, full_down)
    expert_out = whole_out.astype(jnp.bfloat16)
    arrived_grad, expert_out = lax.optimization_barrier((arrived_grad, expert_out))
    row_dots = jnp.sum(
        arrived_grad.astype(jnp.float32) * expert_out.astype(jnp.float32), axis=-1
    ).reshape(local_experts, n_expert, capacity)
    row_dots = lax.all_to_all(
        row_dots.transpose(1, 0, 2), "expert", split_axis=0, concat_axis=0, tiled=True
    )

    grad_act = jnp.einsum(
        "erd,efd->erf", arrived_grad, full_down, preferred_element_type=jnp.float32
    )
    grad_pre = jax.vjp(jax.nn.gelu, pre_act.astype(jnp.float32))[1](grad_act)[0]
    grad_pre = grad_pre.astype(jnp.bfloat16)
    whole_back = jnp.einsum("erf,edf->erd", grad_pre, full_up, preferred_element_type=jnp.float32)
    returned_grad = from_experts(
        whole_back.astype(jnp.bfloat16), n_expert, local_experts, capacity
    )
    whole_down = jnp.einsum(
        "erf,erd->efd", activation, arrived_grad, preferred_element_type=jnp.float32
    ).astype(jnp.bfloat16)
    whole_up = jnp.einsum(
        "erd,erf->edf", arrived, grad_pre, preferred_element_type=jnp.float32
    ).astype(jnp.bfloat16)
    returned_grad, whole_down, whole_up, expert_out = lax.optimization_barrier(
        (returned_grad, whole_down, whole_up, expert_out)
    )
    dw_down = lax.psum_scatter(whole_down, "shard", scatter_dimension=1, tiled=True)
    dw_up = lax.psum_scatter(whole_up, "shard", scatter_dimension=2, tiled=True)
    returned = from_experts(expert_out, n_expert, local_experts, capacity)

    gated = lax.dot_general(
        placing,
        row_dots.reshape(experts * capacity, 1).astype(jnp.bfloat16),
        TN,
        preferred_element_type=jnp.float32,
    )
    grad_logits = (gated * (picked - router)).astype(jnp.bfloat16)
    grad_expert_in = lax.dot_general(
        placing, returned_grad, TN, preferred_element_type=jnp.float32
    )
    dw_router = jnp.einsum("td,te->de", normed_two, grad_logits, preferred_element_type=jnp.float32)
    grad_normed_two = grad_expert_in + jnp.einsum(
        "te,de->td", grad_logits, router_w, preferred_element_type=jnp.float32
    )
    grad_hidden_in, dgain_ffn = rms_back(grad_normed_two, hidden_one, second_scale, gain_two)
    grad_hidden = grad_mixed + grad_hidden_in
    grad_attn = grad_hidden.astype(jnp.bfloat16)
    grad_merged = jnp.einsum(
        "te,de->td", grad_attn, output_w, preferred_element_type=jnp.float32
    ).astype(jnp.bfloat16)

    half = model_width // (2 * PAIR) * PAIR
    spans = ((0, half), (half, model_width - half))
    whole_w = [
        jnp.concatenate([w[:, at : at + size] for w in (query_w, key_w, value_w)], axis=1)
        for at, size in spans
    ]
    one = attend_backward(query, keys, values, grad_merged, probs, head_size, *spans[0])
    grads_one = jnp.concatenate(one[:3], axis=1)
    dw_one = jnp.einsum("td,te->de", normed_one, grads_one, preferred_element_type=jnp.float32)
    dw_output = jnp.einsum("td,te->de", merged, grad_attn, preferred_element_type=jnp.float32)
    dw_one = jnp.concatenate([dw_one.astype(jnp.bfloat16), dw_output.astype(jnp.bfloat16)], axis=1)
    grad_merged, dw_one, dw_down, dw_up = lax.optimization_barrier(
        (grad_merged, dw_one, dw_down, dw_up)
    )
    rows_one = lax.psum_scatter(dw_one, "shard", scatter_dimension=0, tiled=True)
    two = attend_backward(query, keys, values, grad_merged, probs, head_size, *spans[1])
    grads_two = jnp.concatenate(two[:3], axis=1)
    grads_two, returned, rows_one = lax.optimization_barrier((grads_two, returned, rows_one))
    dw_two = jnp.einsum("td,te->de", normed_one, grads_two, preferred_element_type=jnp.float32)

    chosen = lax.dot_general(placing, returned, TN, preferred_element_type=jnp.float32)
    block_out = hidden_one + gate_prob[:, None] * chosen
    grad_normed_one = jnp.einsum(
        "te,de->td", grads_one, whole_w[0], preferred_element_type=jnp.float32
    ) + jnp.einsum("te,de->td", grads_two, whole_w[1], preferred_element_type=jnp.float32)
    grad_stream, dgain_attn = rms_back(grad_normed_one, stream, first_scale, gain_one)
    dtokens = grad_hidden + grad_stream
    folded = jnp.concatenate([one[3], two[3]], axis=0)
    grad_rows = sum(
        jnp.pad(folded[:, row, row:], ((0, 0), (0, row))) for row in range(folded.shape[1])
    )
    dbias_table = jnp.einsum(
        "rb,hr->bh", bucket_onehot.astype(jnp.float32), grad_rows, precision=lax.Precision.HIGHEST
    )
    width = dw_two.shape[1]
    small = jnp.concatenate(
        [
            values_of.reshape(n_shard, -1)
            for values_of in (dw_router, dgain_ffn, dgain_attn, dbias_table)
        ],
        axis=1,
    )
    extra = -(-small.shape[1] // (width * n_expert)) * n_expert
    small = jnp.pad(small, ((0, 0), (0, extra * width - small.shape[1])))
    blocks = jnp.concatenate(
        [
            dw_two.astype(jnp.bfloat16).reshape(n_shard, held, width),
            small.astype(jnp.bfloat16).reshape(n_shard, extra, width),
        ],
        axis=1,
    )
    rows_two = summed_blocks(blocks, "shard")
    sums_one = total_over_experts(rows_one, n_expert)
    sums_two = total_over_experts(rows_two, n_expert)
    parts = [
        jnp.concatenate(
            [
                sums_one[:, place * half : (place + 1) * half],
                sums_two[:held, place * spans[1][1] : (place + 1) * spans[1][1]],
            ],
            axis=1,
        )
        for place in range(3)
    ]
    rest = sums_two[held:].reshape(-1)
    ends = [held * experts, held * (experts + 1), held * (experts + 2)]
    return (
        block_out,
        dtokens,
        rest[ends[1] : ends[2]],
        rest[ends[2] : ends[2] + bias_table.size].reshape(bias_table.shape),
        parts[0],
        parts[1],
        parts[2],
        sums_one[:, 3 * half :],
        rest[ends[0] : ends[1]],
        rest[: ends[0]].reshape(held, experts),
        dw_up.astype(jnp.float32),
        dw_down.astype(jnp.float32),
    )


def solution(mesh):
    placed = (
        P(("expert", "shard"), None),
        P(("expert", "shard")),
        P(("expert", "shard")),
        P(),
        P("shard"),
        P("shard", None),
        P("shard", None),
        P("shard", None),
        P("shard", None),
        P("shard", None),
        P("shard"),
        P("shard", None),
        P("expert", None, "shard"),
        P("expert", "shard", None),
        P(("expert", "shard"), None),
    )
    return jax.shard_map(
        shards,
        mesh=mesh,
        in_specs=placed,
        out_specs=(
            P(("expert", "shard"), None),
            P(("expert", "shard"), None),
            P("shard"),
            P("shard", None),
            P("shard", None),
            P("shard", None),
            P("shard", None),
            P("shard", None),
            P("shard"),
            P("shard", None),
            P("expert", None, "shard"),
            P("expert", "shard", None),
        ),
        check_vma=False,
    )
```
